32 devices in a mesh: grp: 2 (over y), chan: 4 (over z), tm: 2 (over x), sub: 2 (over core).
Axes of the slice: x: 2, y: 2, z: 4, core: 2. Of those that a mesh axis runs over, the one named last changes fastest.
Arguments:
- traces: bfloat16 [1024, 4, 4096], P(('grp', 'chan'), 'tm'), parts along dimension 0
- valid: int32 [1024, 4], P(('grp', 'chan'), 'tm'), parts along dimension 0, may hold values from 0 to 1
- source_channel_index: int32 [8, 32], P(('grp', 'sub')), parts along dimension 0, may hold values from 0 to 511, as said below
Outputs:
- stack: float32 [32, 256, 512], P(None, ('grp', 'sub'), ('chan', 'tm')), parts along dimension 1
The draws below stay inside these ranges and needn't reach their ends.
There are 2 independent parts, one for each index of `grp`. The reference program is written for one: setup_inputs(seed, part) draws one part's arguments, and reference() takes and returns one part's arrays. A program takes and returns all parts, laid end to end along the dimension named above; each array names one. Nothing has to cross between parts.
Inputs may be any that keep to these rules, and one draw needn't show every extreme that they name: `source_channel_index`: the 32 channels of one panel are distinct and lie in one block of 128 channels (b * 128 to b * 128 + 127); different panels lie in different blocks.
All inputs are finite; a program needn't handle non-finite values.
Results may differ from the reference program's by a relative error of at most 0.0003.
Values may be sent and summed in bfloat16 or wider, within the bound.
A program may use at most 64 MiB of HBM per device.

```python
import math
import jax
import jax.numpy as jnp
from jax import lax

RESIDENT_CHANNELS = 128
SAMP = 4096
LAGS = 32
PSRC = 32
PANELS = 4
CHANNELS = 512
SEGS = 4
SOURCES = 128


def draw_traces(key, part):
    first, second, third = jax.random.split(key, 3)
    base = jax.random.normal(first, (CHANNELS, SEGS, SAMP), jnp.float32)
    row_scale = jnp.exp(jax.random.uniform(second, (CHANNELS, SEGS, 1), jnp.float32, -1.2, 1.2))
    col_scale = jnp.exp(jax.random.uniform(third, (1, SEGS, SAMP), jnp.float32, -1.2, 1.2))
    return (base * row_scale * col_scale).astype(jnp.bfloat16)


def draw_valid(key, part):
    segment = jnp.arange(SEGS, dtype=jnp.int32)[None, :]
    limit = 300 + 600 * segment // max(SEGS - 1, 1)
    rolled = jax.random.randint(key, (CHANNELS, SEGS), 0, 1000, dtype=jnp.int32)
    return (rolled < limit).astype(jnp.int32)


def draw_source_channel_index(key, part):
    first, second = jax.random.split(jax.random.fold_in(key, 17))
    owners = jax.random.permutation(first, CHANNELS // RESIDENT_CHANNELS)[:PANELS].astype(jnp.int32)
    panel_keys = jax.random.split(second, PANELS)
    offsets = jax.vmap(lambda inner: jax.random.permutation(inner, RESIDENT_CHANNELS)[:PSRC])(panel_keys).astype(jnp.int32)
    return (owners[:, None] * RESIDENT_CHANNELS + offsets).astype(jnp.int32)


def setup_inputs(seed: int = 0, part: int = 0) -> dict:
    key_list = jax.random.split(jax.random.key(seed), 4)
    part_keys = jax.random.split(jax.random.fold_in(key_list[3], part), 4)
    return {
        "traces": draw_traces(jax.random.fold_in(jax.random.fold_in(key_list[3], part), 71), part),
        "valid": draw_valid(jax.random.fold_in(jax.random.fold_in(key_list[3], part), 71), part),
        "source_channel_index": draw_source_channel_index(jax.random.fold_in(jax.random.fold_in(key_list[3], part), 71), part),
    }


def shifted_block(src, first, count):
    width = src.shape[-1]
    rows = []
    for lag in range(first, first + count):
        rows.append(jnp.pad(src, ((0, 0), (lag, 0)))[:, :width])
    return jnp.stack(rows)

def reference(traces, valid, source_channel_index):
    flat = source_channel_index.reshape(-1)
    sources = traces[flat]
    src_valid = valid[flat].astype(jnp.float32)
    rec_valid = valid.astype(jnp.float32)
    group = min(8, LAGS)
    root = math.sqrt(SAMP)

    def one(acc, k):
        receiver_trace = lax.dynamic_index_in_dim(traces, k, 1, keepdims=False).astype(jnp.float32)
        src = lax.dynamic_index_in_dim(sources, k, 1, keepdims=False).astype(jnp.float32)
        rms_rec = jnp.sqrt(lax.optimization_barrier(jnp.mean(receiver_trace * receiver_trace, axis=1)) + 1e-05)
        rms_src = jnp.sqrt(lax.optimization_barrier(jnp.mean(src * src, axis=1)) + 1e-05)
        mask_rec = lax.dynamic_index_in_dim(rec_valid, k, 1, keepdims=False)
        mask_src = lax.dynamic_index_in_dim(src_valid, k, 1, keepdims=False)
        scale = mask_src[:, None] * mask_rec[None, :] / (root * rms_src[:, None] * rms_rec[None, :])
        blocks = []
        for start in range(0, LAGS, group):
            lag_shifted = shifted_block(src, start, group)
            lagged_product = jnp.einsum('ncd,id->nci', lag_shifted, receiver_trace, precision=lax.Precision.HIGHEST)
            blocks.append(lagged_product * scale[None])
        return (acc + jnp.concatenate(blocks, axis=0), None)
    init = jnp.zeros((LAGS, SOURCES, CHANNELS), jnp.float32)
    summed, _ = lax.scan(one, init, jnp.arange(SEGS, dtype=jnp.int32))
    pairs = jnp.dot(src_valid, rec_valid.T, precision=lax.Precision.HIGHEST)
    return summed / jnp.sqrt(jnp.maximum(pairs, 1.0))[None]
```

```python
import functools
import math

import jax
import jax.numpy as jnp
from jax import lax
from jax.experimental import pallas as pl
from jax.experimental.pallas import tpu as pltpu
from jax.sharding import PartitionSpec as P

LAGS = 32
SRC_SHIFTS = 8
REC_SHIFTS = LAGS // SRC_SHIFTS
LANES = 128
MESH = pl.DeviceIdType.MESH


def from_root(array, axis, root):
    size = lax.axis_size(axis)
    moving = jnp.where(lax.axis_index(axis) == root, array, jnp.zeros_like(array))
    total = moving
    for _ in range(size - 1):
        moving = lax.ppermute(moving, axis, [(i, (i + 1) % size) for i in range(size)])
        total = total + moving
    return total


def sum_to_owners(array, axis, dim):
    size = lax.axis_size(axis)
    part = array.shape[dim] // size
    me = lax.axis_index(axis)

    def piece(owner):
        return lax.dynamic_slice_in_dim(array, owner * part, part, dim)

    total = piece(me)
    for step in range(1, size):
        away = [(i, (i + step) % size) for i in range(size)]
        total = total + lax.ppermute(piece((me + step) % size), axis, away)
    return total


def shifted_block(src, first, count):
    width = src.shape[-1]
    rows = []
    for lag in range(first, first + count):
        rows.append(jnp.pad(src, ((0, 0), (0, 0), (lag, 0)))[:, :, :width])
    return jnp.stack(rows)


def general_body(traces, valid, source_channel_index):
    resident_traces = traces.shape[0]
    seg_here = traces.shape[1]
    width = traces.shape[2]
    panels_here = source_channel_index.shape[0]
    per_panel = source_channel_index.shape[1]
    rms_rec = jnp.sqrt(jnp.mean(jnp.square(traces.astype(jnp.float32)), axis=2) + 1e-05)
    rec_mask = valid.astype(jnp.float32)
    owners = source_channel_index[:, 0] // resident_traces
    local_rows = (source_channel_index - owners[:, None] * resident_traces).reshape(-1)
    picked = traces[local_rows].reshape(panels_here, per_panel, seg_here, width)
    pick_mask = valid[local_rows].reshape(panels_here, per_panel, seg_here).astype(jnp.bfloat16)

    def fetch(panel):
        return (
            from_root(picked[panel], "chan", owners[panel]),
            from_root(pick_mask[panel], "chan", owners[panel]),
        )

    fetched = [fetch(panel) for panel in range(panels_here)]
    sources = jnp.stack([item[0] for item in fetched])
    src_flags = jnp.stack([item[1] for item in fetched])
    sources = sources.reshape(panels_here * per_panel, seg_here, width)
    src_mask = src_flags.reshape(panels_here * per_panel, seg_here).astype(jnp.float32)
    rms_src = jnp.sqrt(jnp.mean(jnp.square(sources.astype(jnp.float32)), axis=2) + 1e-05)
    scale = (
        src_mask.T[:, :, None]
        * rec_mask.T[:, None, :]
        / (math.sqrt(width) * rms_src.T[:, :, None] * rms_rec.T[:, None, :])
    )
    group = min(8, LAGS)
    blocks = []
    for start in range(0, LAGS, group):
        lag_shifted = shifted_block(sources, start, group)
        lagged_product = jnp.einsum(
            "lsku,rku->klsr", lag_shifted, traces, preferred_element_type=jnp.float32
        )
        blocks.append(jnp.sum(lagged_product * scale[:, None], axis=0))
    partial_stack_value = jnp.concatenate(blocks, axis=0)
    pair_terms = jnp.dot(src_mask, rec_mask.T, preferred_element_type=jnp.float32)
    total = sum_to_owners(partial_stack_value, "tm", 2)
    pairs = sum_to_owners(pair_terms, "tm", 1)
    return total / jnp.sqrt(jnp.maximum(pairs, 1.0))[None]


def kernel(
    n_chan, x_ref, idx_ref, val_ref, out_ref,
    slots, idx_sib, shifted_rec, shifted_src, wrow, vrow, own, xsend, xrecv, fin, finr,
    idx_sems, z_send, z_recv, s_send, s_recv, x_send, x_recv, f_send, f_recv,
):
    segs, resident, width = x_ref.shape
    per = idx_ref.shape[0] // 2
    q = resident // 4
    z = lax.axis_index("chan")
    x = lax.axis_index("tm")
    k = lax.axis_index("sub")
    has_left = z > 0
    has_right = z < n_chan - 1

    barrier = pltpu.get_barrier_semaphore()
    pl.semaphore_signal(barrier, inc=1, device_id={"sub": 1 - k}, device_id_type=MESH)
    pl.semaphore_signal(barrier, inc=1, device_id={"tm": 1 - x}, device_id_type=MESH)

    @pl.when(has_left)
    def _():
        pl.semaphore_signal(barrier, inc=1, device_id={"chan": z - 1}, device_id_type=MESH)

    @pl.when(has_right)
    def _():
        pl.semaphore_signal(barrier, inc=1, device_id={"chan": z + 1}, device_id_type=MESH)

    pl.semaphore_wait(barrier, 2 + has_left.astype(jnp.int32) + has_right.astype(jnp.int32))

    def remote(src, dst, send, recv, where):
        return pltpu.make_async_remote_copy(
            src_ref=src, dst_ref=dst, send_sem=send, recv_sem=recv,
            device_id=where, device_id_type=MESH,
        )

    def z_copy(b, right):
        step = 1 if right else -1
        part = slots.at[b, k]
        return remote(part, part, z_send.at[b, int(right)], z_recv.at[b], {"chan": z + step})

    def s_copy(b, seg):
        part = slots.at[b, seg]
        return remote(part, part, s_send.at[b], s_recv.at[b], {"sub": 1 - k})

    def x_copy(b):
        return remote(xsend.at[b], xrecv.at[b], x_send.at[b], x_recv.at[b], {"tm": 1 - x})

    def f_copy(b):
        return remote(fin.at[b], finr.at[b], f_send.at[b], f_recv.at[b], {"sub": 1 - k})

    idx_copy = remote(idx_ref, idx_sib, idx_sems.at[0], idx_sems.at[1], {"sub": 1 - k})
    idx_copy.start()
    idx_copy.wait()

    lane = lax.broadcasted_iota(jnp.int32, (per, resident), 1)
    sel = jnp.zeros((per, resident), jnp.float32)
    for ref in (idx_ref, idx_sib):
        for p in range(2):
            hit = ref[p * per : (p + 1) * per, :] - z * resident == lane
            sel = sel + jnp.where(hit, 1.0, 0.0)
    sel = sel.astype(jnp.bfloat16)
    tile = 1024
    for t in range(0, width, tile):
        slots[z, k, :, t : t + tile] = jnp.dot(
            sel, x_ref[k, :, t : t + tile], preferred_element_type=jnp.float32
        ).astype(jnp.bfloat16)
    slots[z, k, :, width:] = jnp.dot(
        sel, val_ref[k].astype(jnp.bfloat16), preferred_element_type=jnp.float32
    ).astype(jnp.bfloat16)

    @pl.when(has_left)
    def _():
        z_copy(z, False).start()

    @pl.when(has_right)
    def _():
        z_copy(z, True).start()

    s_copy(z, k).start()

    wide = lax.broadcasted_iota(jnp.int32, (q, width), 1)
    for seg in range(segs):
        wcols, vcols = [], []
        for half in range(2):
            side = x if half == 0 else 1 - x
            first = pl.multiple_of(side * (2 * q) + k * q, q)
            rec = x_ref[seg, pl.ds(first, q), :].astype(jnp.float32)
            flag = val_ref[seg, pl.ds(first, q), :]
            mean = jnp.sum(rec * rec, axis=1, keepdims=True) * (1.0 / width)
            w = flag / jnp.sqrt(mean + 1e-05)
            for h in range(REC_SHIFTS):
                by = SRC_SHIFTS * h
                moved = rec
                if by:
                    moved = jnp.where(wide < width - by, pltpu.roll(rec, width - by, 1), 0.0)
                row = (half * REC_SHIFTS + h) * q
                shifted_rec[seg, row : row + q, :] = moved.astype(jnp.bfloat16)
                wcols.append(w)
                vcols.append(flag)
        wrow[seg] = jnp.concatenate(wcols, axis=0).T[:per]
        vrow[seg] = jnp.concatenate(vcols, axis=0).T[:per]

    def compute(b):
        s_copy(b, 1 - k).wait_recv()
        acc = None
        pairs = None
        for seg in range(segs):
            src = slots[b, seg, :, :width].astype(jnp.float32)
            flag = slots[b, seg, :, width:].astype(jnp.float32)
            mean = jnp.sum(src * src, axis=1, keepdims=True) * (1.0 / width)
            a = flag / (math.sqrt(width) * jnp.sqrt(mean + 1e-05))
            a = jnp.concatenate([a, a], axis=1)
            f = jnp.concatenate([flag, flag], axis=1)
            for j in range(SRC_SHIFTS):
                moved = src
                if j:
                    moved = jnp.where(wide[:per] >= j, pltpu.roll(src, j, 1), 0.0)
                shifted_src[seg, j * per : (j + 1) * per, :] = moved.astype(jnp.bfloat16)
            d = lax.dot_general(
                shifted_src[seg], shifted_rec[seg], (((1,), (1,)), ((), ())),
                preferred_element_type=jnp.float32,
            )
            term = d.reshape(SRC_SHIFTS, per, 2 * LANES) * (a * wrow[seg])[None]
            pair = f * vrow[seg]
            acc = term if acc is None else acc + term
            pairs = pair if pairs is None else pairs + pair
        rows = SRC_SHIFTS * per
        own[b, :rows] = acc[:, :, :LANES].reshape(rows, LANES)
        own[b, rows:] = pairs[:, :LANES]
        xsend[b, :rows] = acc[:, :, LANES:].reshape(rows, LANES)
        xsend[b, rows:] = pairs[:, LANES:]
        x_copy(b).start()

    def finish(b):
        x_copy(b).wait_recv()
        rows = SRC_SHIFTS * per
        total = own[b, :rows] + xrecv[b, :rows]
        pairs = own[b, rows:] + xrecv[b, rows:]
        norm = 1.0 / jnp.sqrt(jnp.maximum(pairs, 1.0))
        fin[b] = (total.reshape(SRC_SHIFTS, per, LANES) * norm[None]).reshape(rows, LANES)
        f_copy(b).start()

    def final(b):
        f_copy(b).wait_recv()
        rows = SRC_SHIFTS * per
        mine, other = fin[b], finr[b]
        low = jnp.where(k == 0, mine, other)
        high = jnp.where(k == 0, other, mine)
        at = lax.broadcasted_iota(jnp.int32, (rows, LANES), 1)
        for h in range(REC_SHIFTS):
            lo = pltpu.roll(low, (LANES - h * q) % LANES, 1) if h else low
            hi = pltpu.roll(high, (LANES + q - h * q) % LANES, 1) if h != 1 else high
            both = jnp.where(at < q, lo, hi)[:, : 2 * q]
            out_ref[b, h * SRC_SHIFTS : (h + 1) * SRC_SHIFTS] = both.reshape(SRC_SHIFTS, per, 2 * q)

    def item(d, way):
        b = z + d * (2 * way - 1)
        ok = (b >= 0) & (b < n_chan) & (d >= 0) & ((d > 0) | (way == 0))
        return b, ok

    @pl.loop(0, n_chan + 2)
    def _(d):
        from_left, ok_left = item(d, 0)
        from_right, ok_right = item(d, 1)

        @pl.when(ok_left & (d > 0))
        def _():
            z_copy(from_left, True).wait_recv()

            @pl.when(has_right)
            def _():
                z_copy(from_left, True).start()

            s_copy(from_left, k).start()

        @pl.when(ok_right & (d > 0))
        def _():
            z_copy(from_right, False).wait_recv()

            @pl.when(has_left)
            def _():
                z_copy(from_right, False).start()

            s_copy(from_right, k).start()

        @pl.loop(0, 2)
        def _(way):
            b, ok = item(d, way)

            @pl.when(ok)
            def _():
                compute(b)

            b1, ok1 = item(d - 1, way)

            @pl.when(ok1)
            def _():
                finish(b1)

            b2, ok2 = item(d - 2, way)

            @pl.when(ok2)
            def _():
                final(b2)

    @pl.loop(0, n_chan)
    def _(b):
        @pl.when(has_left & (b >= z))
        def _():
            z_copy(b, False).wait_send()

        @pl.when(has_right & (b <= z))
        def _():
            z_copy(b, True).wait_send()

        s_copy(b, k).wait_send()
        x_copy(b).wait_send()
        f_copy(b).wait_send()


def fast_body(n_chan, traces, valid, source_channel_index):
    resident, segs, width = traces.shape
    panels, per = source_channel_index.shape
    x = jnp.transpose(traces, (1, 0, 2))
    idx = jnp.broadcast_to(source_channel_index.reshape(-1)[:, None], (panels * per, LANES))
    val = jnp.broadcast_to(valid.T.astype(jnp.float32)[:, :, None], (segs, resident, LANES))
    rows = SRC_SHIFTS * per
    vmem = pl.BlockSpec(memory_space=pltpu.VMEM)
    dma = pltpu.SemaphoreType.DMA
    f32, bf16 = jnp.float32, jnp.bfloat16
    found = pl.pallas_call(
        functools.partial(kernel, n_chan),
        out_shape=jax.ShapeDtypeStruct((n_chan, LAGS, per, resident // 2), f32),
        in_specs=[vmem] * 3,
        out_specs=vmem,
        scratch_shapes=[
            pltpu.VMEM((n_chan, segs, per, width + LANES), bf16),
            pltpu.VMEM((panels * per, LANES), jnp.int32),
            pltpu.VMEM((segs, 2 * LANES, width), bf16),
            pltpu.VMEM((segs, rows, width), bf16),
            pltpu.VMEM((segs, per, 2 * LANES), f32),
            pltpu.VMEM((segs, per, 2 * LANES), f32),
            pltpu.VMEM((n_chan, rows + per, LANES), f32),
            pltpu.VMEM((n_chan, rows + per, LANES), f32),
            pltpu.VMEM((n_chan, rows + per, LANES), f32),
            pltpu.VMEM((n_chan, rows, LANES), f32),
            pltpu.VMEM((n_chan, rows, LANES), f32),
            dma((2,)),
            dma((n_chan, 2)),
            dma((n_chan,)),
            dma((n_chan,)),
            dma((n_chan,)),
            dma((n_chan,)),
            dma((n_chan,)),
            dma((n_chan,)),
            dma((n_chan,)),
        ],
        compiler_params=pltpu.CompilerParams(
            collective_id=0, has_side_effects=True, vmem_limit_bytes=48 * 1024 * 1024
        ),
    )(x, idx, val)
    owners = source_channel_index[:, 0] // resident
    return jnp.concatenate(
        [lax.dynamic_index_in_dim(found, owners[p], 0, keepdims=False) for p in range(panels)], axis=1
    )


def solution(mesh):
    in_specs = (P(("grp", "chan"), "tm", None), P(("grp", "chan"), "tm"), P(("grp", "sub"), None))
    out_specs = P(None, ("grp", "sub"), ("chan", "tm"))
    size = mesh.shape

    def body(traces, valid, source_channel_index):
        panels = source_channel_index.shape[0] * size["sub"]
        fits = (
            (size["tm"], size["sub"], traces.shape[1]) == (2, 2, 2)
            and panels == size["chan"]
            and traces.shape[0] == LANES
            and source_channel_index.shape == (2, LANES // REC_SHIFTS)
        )
        if fits:
            return fast_body(size["chan"], traces, valid, source_channel_index)
        return general_body(traces, valid, source_channel_index)

    return jax.shard_map(body, mesh=mesh, in_specs=in_specs, out_specs=out_specs, check_vma=False)
```

```python
import functools
import math

import jax
import jax.numpy as jnp
from jax import lax
from jax.experimental import pallas as pl
from jax.experimental.pallas import tpu as pltpu
from jax.sharding import PartitionSpec as P

LAGS = 32
SRC_SHIFTS = 8
REC_SHIFTS = LAGS // SRC_SHIFTS
LANES = 128
MESH = pl.DeviceIdType.MESH


def from_root(array, axis, root):
    size = lax.axis_size(axis)
    moving = jnp.where(lax.axis_index(axis) == root, array, jnp.zeros_like(array))
    total = moving
    for _ in range(size - 1):
        moving = lax.ppermute(moving, axis, [(i, (i + 1) % size) for i in range(size)])
        total = total + moving
    return total


def sum_to_owners(array, axis, dim):
    size = lax.axis_size(axis)
    part = array.shape[dim] // size
    me = lax.axis_index(axis)

    def piece(owner):
        return lax.dynamic_slice_in_dim(array, owner * part, part, dim)

    total = piece(me)
    for step in range(1, size):
        away = [(i, (i + step) % size) for i in range(size)]
        total = total + lax.ppermute(piece((me + step) % size), axis, away)
    return total


def shifted_block(src, first, count):
    width = src.shape[-1]
    rows = []
    for lag in range(first, first + count):
        rows.append(jnp.pad(src, ((0, 0), (0, 0), (lag, 0)))[:, :, :width])
    return jnp.stack(rows)


def general_body(traces, valid, source_channel_index):
    resident_traces = traces.shape[0]
    seg_here = traces.shape[1]
    width = traces.shape[2]
    panels_here = source_channel_index.shape[0]
    per_panel = source_channel_index.shape[1]
    rms_rec = jnp.sqrt(jnp.mean(jnp.square(traces.astype(jnp.float32)), axis=2) + 1e-05)
    rec_mask = valid.astype(jnp.float32)
    owners = source_channel_index[:, 0] // resident_traces
    local_rows = (source_channel_index - owners[:, None] * resident_traces).reshape(-1)
    chosen = (local_rows[:, None] == jnp.arange(resident_traces)[None, :]).astype(jnp.bfloat16)
    picked = jnp.einsum("nc,ckt->nkt", chosen, traces, preferred_element_type=jnp.float32)
    picked = picked.astype(jnp.bfloat16).reshape(panels_here, per_panel, seg_here, width)
    pick_mask = jnp.dot(chosen, valid.astype(jnp.bfloat16), preferred_element_type=jnp.float32)
    pick_mask = pick_mask.astype(jnp.bfloat16).reshape(panels_here, per_panel, seg_here)

    def fetch(panel):
        return (
            from_root(picked[panel], "chan", owners[panel]),
            from_root(pick_mask[panel], "chan", owners[panel]),
        )

    fetched = [fetch(panel) for panel in range(panels_here)]
    sources = jnp.stack([item[0] for item in fetched])
    src_flags = jnp.stack([item[1] for item in fetched])
    sources = sources.reshape(panels_here * per_panel, seg_here, width)
    src_mask = src_flags.reshape(panels_here * per_panel, seg_here).astype(jnp.float32)
    rms_src = jnp.sqrt(jnp.mean(jnp.square(sources.astype(jnp.float32)), axis=2) + 1e-05)
    scale = (
        src_mask.T[:, :, None]
        * rec_mask.T[:, None, :]
        / (math.sqrt(width) * rms_src.T[:, :, None] * rms_rec.T[:, None, :])
    )
    group = min(8, LAGS)
    blocks = []
    for start in range(0, LAGS, group):
        lag_shifted = shifted_block(sources, start, group)
        lagged_product = jnp.einsum(
            "lsku,rku->klsr", lag_shifted, traces, preferred_element_type=jnp.float32
        )
        blocks.append(jnp.sum(lagged_product * scale[:, None], axis=0))
    partial_stack_value = jnp.concatenate(blocks, axis=0)
    pair_terms = jnp.dot(src_mask, rec_mask.T, preferred_element_type=jnp.float32)
    total = sum_to_owners(partial_stack_value, "tm", 2)
    pairs = sum_to_owners(pair_terms, "tm", 1)
    return total / jnp.sqrt(jnp.maximum(pairs, 1.0))[None]


def kernel(
    n_chan, x_ref, idx_ref, val_ref, out_ref,
    slots, idx_sib, shifted_rec, shifted_src, wrow, vrow, own, xsend, xrecv, fin, finr,
    idx_sems, z_send, z_recv, s_send, s_recv, x_send, x_recv, f_send, f_recv,
):
    segs, resident, width = x_ref.shape
    per = idx_ref.shape[0] // 2
    q = resident // 4
    z = lax.axis_index("chan")
    x = lax.axis_index("tm")
    k = lax.axis_index("sub")
    has_left = z > 0
    has_right = z < n_chan - 1

    barrier = pltpu.get_barrier_semaphore()
    pl.semaphore_signal(barrier, inc=1, device_id={"sub": 1 - k}, device_id_type=MESH)
    pl.semaphore_signal(barrier, inc=1, device_id={"tm": 1 - x}, device_id_type=MESH)

    @pl.when(has_left)
    def _():
        pl.semaphore_signal(barrier, inc=1, device_id={"chan": z - 1}, device_id_type=MESH)

    @pl.when(has_right)
    def _():
        pl.semaphore_signal(barrier, inc=1, device_id={"chan": z + 1}, device_id_type=MESH)

    pl.semaphore_wait(barrier, 2 + has_left.astype(jnp.int32) + has_right.astype(jnp.int32))

    def remote(src, dst, send, recv, where):
        return pltpu.make_async_remote_copy(
            src_ref=src, dst_ref=dst, send_sem=send, recv_sem=recv,
            device_id=where, device_id_type=MESH,
        )

    def z_copy(b, right):
        step = 1 if right else -1
        part = slots.at[b, k]
        return remote(part, part, z_send.at[b, int(right)], z_recv.at[b], {"chan": z + step})

    def s_copy(b, seg):
        part = slots.at[b, seg]
        return remote(part, part, s_send.at[b], s_recv.at[b], {"sub": 1 - k})

    def x_copy(b):
        return remote(xsend.at[b], xrecv.at[b], x_send.at[b], x_recv.at[b], {"tm": 1 - x})

    def f_copy(b):
        return remote(fin.at[b], finr.at[b], f_send.at[b], f_recv.at[b], {"sub": 1 - k})

    idx_copy = remote(idx_ref, idx_sib, idx_sems.at[0], idx_sems.at[1], {"sub": 1 - k})
    idx_copy.start()
    idx_copy.wait()

    lane = lax.broadcasted_iota(jnp.int32, (per, resident), 1)
    sel = jnp.zeros((per, resident), jnp.float32)
    for ref in (idx_ref, idx_sib):
        for p in range(2):
            hit = ref[p * per : (p + 1) * per, :] - z * resident == lane
            sel = sel + jnp.where(hit, 1.0, 0.0)
    sel = sel.astype(jnp.bfloat16)
    tile = 1024
    for t in range(0, width, tile):
        slots[z, k, :, t : t + tile] = jnp.dot(
            sel, x_ref[k, :, t : t + tile], preferred_element_type=jnp.float32
        ).astype(jnp.bfloat16)
    slots[z, k, :, width:] = jnp.dot(
        sel, val_ref[k].astype(jnp.bfloat16), preferred_element_type=jnp.float32
    ).astype(jnp.bfloat16)

    @pl.when(has_left)
    def _():
        z_copy(z, False).start()

    @pl.when(has_right)
    def _():
        z_copy(z, True).start()

    s_copy(z, k).start()

    out_ref[...] = jnp.zeros_like(out_ref)
    wide = lax.broadcasted_iota(jnp.int32, (q, width), 1)
    for seg in range(segs):
        wcols, vcols = [], []
        for half in range(2):
            side = x if half == 0 else 1 - x
            first = pl.multiple_of(side * (2 * q) + k * q, q)
            rec = x_ref[seg, pl.ds(first, q), :].astype(jnp.float32)
            flag = val_ref[seg, pl.ds(first, q), :]
            mean = jnp.sum(rec * rec, axis=1, keepdims=True) * (1.0 / width)
            w = flag / jnp.sqrt(mean + 1e-05)
            for h in range(REC_SHIFTS):
                by = SRC_SHIFTS * h
                moved = rec
                if by:
                    moved = jnp.where(wide < width - by, pltpu.roll(rec, width - by, 1), 0.0)
                row = (half * REC_SHIFTS + h) * q
                shifted_rec[seg, row : row + q, :] = moved.astype(jnp.bfloat16)
                wcols.append(w)
                vcols.append(flag)
        wrow[seg] = jnp.concatenate(wcols, axis=0).T[:per]
        vrow[seg] = jnp.concatenate(vcols, axis=0).T[:per]

    def compute(b):
        s_copy(b, 1 - k).wait_recv()
        acc = None
        pairs = None
        for seg in range(segs):
            src = slots[b, seg, :, :width].astype(jnp.float32)
            flag = slots[b, seg, :, width:].astype(jnp.float32)
            mean = jnp.sum(src * src, axis=1, keepdims=True) * (1.0 / width)
            a = flag / (math.sqrt(width) * jnp.sqrt(mean + 1e-05))
            a = jnp.concatenate([a, a], axis=1)
            f = jnp.concatenate([flag, flag], axis=1)
            for j in range(SRC_SHIFTS):
                moved = src
                if j:
                    moved = jnp.where(wide[:per] >= j, pltpu.roll(src, j, 1), 0.0)
                shifted_src[seg, j * per : (j + 1) * per, :] = moved.astype(jnp.bfloat16)
            d = lax.dot_general(
                shifted_src[seg], shifted_rec[seg], (((1,), (1,)), ((), ())),
                preferred_element_type=jnp.float32,
            )
            term = d.reshape(SRC_SHIFTS, per, 2 * LANES) * (a * wrow[seg])[None]
            pair = f * vrow[seg]
            acc = term if acc is None else acc + term
            pairs = pair if pairs is None else pairs + pair
        rows = SRC_SHIFTS * per
        own[b, :rows] = acc[:, :, :LANES].reshape(rows, LANES)
        own[b, rows:] = pairs[:, :LANES]
        xsend[b, :rows] = acc[:, :, LANES:].reshape(rows, LANES)
        xsend[b, rows:] = pairs[:, LANES:]
        x_copy(b).start()

    def finish(b):
        x_copy(b).wait_recv()
        rows = SRC_SHIFTS * per
        total = own[b, :rows] + xrecv[b, :rows]
        pairs = own[b, rows:] + xrecv[b, rows:]
        norm = 1.0 / jnp.sqrt(jnp.maximum(pairs, 1.0))
        fin[b] = (total.reshape(SRC_SHIFTS, per, LANES) * norm[None]).reshape(rows, LANES)
        f_copy(b).start()

    def final(b):
        f_copy(b).wait_recv()
        rows = SRC_SHIFTS * per
        mine, other = fin[b], finr[b]
        low = jnp.where(k == 0, mine, other)
        high = jnp.where(k == 0, other, mine)
        at = lax.broadcasted_iota(jnp.int32, (rows, LANES), 1)
        for h in range(REC_SHIFTS):
            lo = pltpu.roll(low, (LANES - h * q) % LANES, 1) if h else low
            hi = pltpu.roll(high, (LANES + q - h * q) % LANES, 1) if h != 1 else high
            both = jnp.where(at < q, lo, hi)[:, : 2 * q]
            both = both.reshape(SRC_SHIFTS, per, 2 * q)
            for p in range(2):
                channel = idx_ref[p * per : (p + 1) * per, : 2 * q]
                held = (channel >= b * resident) & (channel < (b + 1) * resident)
                at_lags = pl.ds(h * SRC_SHIFTS, SRC_SHIFTS)
                at_rows = pl.ds(p * per, per)
                before = out_ref[at_lags, at_rows, :]
                out_ref[at_lags, at_rows, :] = jnp.where(held[None], both, before)

    def item(d, way):
        b = z + d * (2 * way - 1)
        ok = (b >= 0) & (b < n_chan) & (d >= 0) & ((d > 0) | (way == 0))
        return b, ok

    @pl.loop(0, n_chan + 2)
    def _(d):
        from_left, ok_left = item(d, 0)
        from_right, ok_right = item(d, 1)

        @pl.when(ok_left & (d > 0))
        def _():
            z_copy(from_left, True).wait_recv()

            @pl.when(has_right)
            def _():
                z_copy(from_left, True).start()

            s_copy(from_left, k).start()

        @pl.when(ok_right & (d > 0))
        def _():
            z_copy(from_right, False).wait_recv()

            @pl.when(has_left)
            def _():
                z_copy(from_right, False).start()

            s_copy(from_right, k).start()

        @pl.loop(0, 2)
        def _(way):
            b, ok = item(d, way)

            @pl.when(ok)
            def _():
                compute(b)

            b1, ok1 = item(d - 1, way)

            @pl.when(ok1)
            def _():
                finish(b1)

            b2, ok2 = item(d - 2, way)

            @pl.when(ok2)
            def _():
                final(b2)

    @pl.loop(0, n_chan)
    def _(b):
        @pl.when(has_left & (b >= z))
        def _():
            z_copy(b, False).wait_send()

        @pl.when(has_right & (b <= z))
        def _():
            z_copy(b, True).wait_send()

        s_copy(b, k).wait_send()
        x_copy(b).wait_send()
        f_copy(b).wait_send()


def fast_body(n_chan, traces, valid, source_channel_index):
    resident, segs, width = traces.shape
    panels, per = source_channel_index.shape
    x = jnp.transpose(traces, (1, 0, 2))
    idx = jnp.broadcast_to(source_channel_index.reshape(-1)[:, None], (panels * per, LANES))
    val = jnp.broadcast_to(valid.T.astype(jnp.float32)[:, :, None], (segs, resident, LANES))
    rows = SRC_SHIFTS * per
    vmem = pl.BlockSpec(memory_space=pltpu.VMEM)
    dma = pltpu.SemaphoreType.DMA
    f32, bf16 = jnp.float32, jnp.bfloat16
    return pl.pallas_call(
        functools.partial(kernel, n_chan),
        out_shape=jax.ShapeDtypeStruct((LAGS, panels * per, resident // 2), f32),
        in_specs=[vmem] * 3,
        out_specs=vmem,
        scratch_shapes=[
            pltpu.VMEM((n_chan, segs, per, width + LANES), bf16),
            pltpu.VMEM((panels * per, LANES), jnp.int32),
            pltpu.VMEM((segs, 2 * LANES, width), bf16),
            pltpu.VMEM((segs, rows, width), bf16),
            pltpu.VMEM((segs, per, 2 * LANES), f32),
            pltpu.VMEM((segs, per, 2 * LANES), f32),
            pltpu.VMEM((n_chan, rows + per, LANES), f32),
            pltpu.VMEM((n_chan, rows + per, LANES), f32),
            pltpu.VMEM((n_chan, rows + per, LANES), f32),
            pltpu.VMEM((n_chan, rows, LANES), f32),
            pltpu.VMEM((n_chan, rows, LANES), f32),
            dma((2,)),
            dma((n_chan, 2)),
            dma((n_chan,)),
            dma((n_chan,)),
            dma((n_chan,)),
            dma((n_chan,)),
            dma((n_chan,)),
            dma((n_chan,)),
            dma((n_chan,)),
        ],
        compiler_params=pltpu.CompilerParams(
            collective_id=0, has_side_effects=True, vmem_limit_bytes=48 * 1024 * 1024
        ),
    )(x, idx, val)


def solution(mesh):
    in_specs = (P(("grp", "chan"), "tm", None), P(("grp", "chan"), "tm"), P(("grp", "sub"), None))
    out_specs = P(None, ("grp", "sub"), ("chan", "tm"))
    size = mesh.shape

    def body(traces, valid, source_channel_index):
        panels = source_channel_index.shape[0] * size["sub"]
        fits = (
            (size["tm"], size["sub"], traces.shape[1]) == (2, 2, 2)
            and panels == size["chan"]
            and traces.shape[0] == LANES
            and source_channel_index.shape == (2, LANES // REC_SHIFTS)
        )
        if fits:
            return fast_body(size["chan"], traces, valid, source_channel_index)
        return general_body(traces, valid, source_channel_index)

    return jax.shard_map(body, mesh=mesh, in_specs=in_specs, out_specs=out_specs, check_vma=False)
```

```python
import functools
import math

import jax
import jax.numpy as jnp
from jax import lax
from jax.experimental import pallas as pl
from jax.experimental.pallas import tpu as pltpu
from jax.sharding import PartitionSpec as P

LAGS = 32
SRC_SHIFTS = 8
REC_SHIFTS = LAGS // SRC_SHIFTS
LANES = 128
MESH = pl.DeviceIdType.MESH


def from_root(array, axis, root):
    size = lax.axis_size(axis)
    moving = jnp.where(lax.axis_index(axis) == root, array, jnp.zeros_like(array))
    total = moving
    for _ in range(size - 1):
        moving = lax.ppermute(moving, axis, [(i, (i + 1) % size) for i in range(size)])
        total = total + moving
    return total


def sum_to_owners(array, axis, dim):
    size = lax.axis_size(axis)
    part = array.shape[dim] // size
    me = lax.axis_index(axis)

    def piece(owner):
        return lax.dynamic_slice_in_dim(array, owner * part, part, dim)

    total = piece(me)
    for step in range(1, size):
        away = [(i, (i + step) % size) for i in range(size)]
        total = total + lax.ppermute(piece((me + step) % size), axis, away)
    return total


def shifted_block(src, first, count):
    width = src.shape[-1]
    rows = []
    for lag in range(first, first + count):
        rows.append(jnp.pad(src, ((0, 0), (0, 0), (lag, 0)))[:, :, :width])
    return jnp.stack(rows)


def general_body(traces, valid, source_channel_index):
    resident_traces = traces.shape[0]
    seg_here = traces.shape[1]
    width = traces.shape[2]
    panels_here = source_channel_index.shape[0]
    per_panel = source_channel_index.shape[1]
    rms_rec = jnp.sqrt(jnp.mean(jnp.square(traces.astype(jnp.float32)), axis=2) + 1e-05)
    rec_mask = valid.astype(jnp.float32)
    owners = source_channel_index[:, 0] // resident_traces
    local_rows = (source_channel_index - owners[:, None] * resident_traces).reshape(-1)
    chosen = (local_rows[:, None] == jnp.arange(resident_traces)[None, :]).astype(jnp.bfloat16)
    picked = jnp.einsum("nc,ckt->nkt", chosen, traces, preferred_element_type=jnp.float32)
    picked = picked.astype(jnp.bfloat16).reshape(panels_here, per_panel, seg_here, width)
    pick_mask = jnp.dot(chosen, valid.astype(jnp.bfloat16), preferred_element_type=jnp.float32)
    pick_mask = pick_mask.astype(jnp.bfloat16).reshape(panels_here, per_panel, seg_here)

    def fetch(panel):
        return (
            from_root(picked[panel], "chan", owners[panel]),
            from_root(pick_mask[panel], "chan", owners[panel]),
        )

    fetched = [fetch(panel) for panel in range(panels_here)]
    sources = jnp.stack([item[0] for item in fetched])
    src_flags = jnp.stack([item[1] for item in fetched])
    sources = sources.reshape(panels_here * per_panel, seg_here, width)
    src_mask = src_flags.reshape(panels_here * per_panel, seg_here).astype(jnp.float32)
    rms_src = jnp.sqrt(jnp.mean(jnp.square(sources.astype(jnp.float32)), axis=2) + 1e-05)
    scale = (
        src_mask.T[:, :, None]
        * rec_mask.T[:, None, :]
        / (math.sqrt(width) * rms_src.T[:, :, None] * rms_rec.T[:, None, :])
    )
    group = min(8, LAGS)
    blocks = []
    for start in range(0, LAGS, group):
        lag_shifted = shifted_block(sources, start, group)
        lagged_product = jnp.einsum(
            "lsku,rku->klsr", lag_shifted, traces, preferred_element_type=jnp.float32
        )
        blocks.append(jnp.sum(lagged_product * scale[:, None], axis=0))
    partial_stack_value = jnp.concatenate(blocks, axis=0)
    pair_terms = jnp.dot(src_mask, rec_mask.T, preferred_element_type=jnp.float32)
    total = sum_to_owners(partial_stack_value, "tm", 2)
    pairs = sum_to_owners(pair_terms, "tm", 1)
    return total / jnp.sqrt(jnp.maximum(pairs, 1.0))[None]


def kernel(
    n_chan, x_ref, idx_ref, val_ref, out_ref,
    slots, idx_sib, shifted_rec, shifted_src, wrow, vrow, own, xsend, xrecv, fin, finr,
    idx_sems, z_send, z_recv, s_send, s_recv, x_send, x_recv, f_send, f_recv,
):
    segs, resident, width = x_ref.shape
    per = idx_ref.shape[0] // 2
    q = resident // 4
    z = lax.axis_index("chan")
    x = lax.axis_index("tm")
    k = lax.axis_index("sub")
    has_left = z > 0
    has_right = z < n_chan - 1

    barrier = pltpu.get_barrier_semaphore()
    pl.semaphore_signal(barrier, inc=1, device_id={"sub": 1 - k}, device_id_type=MESH)
    pl.semaphore_signal(barrier, inc=1, device_id={"tm": 1 - x}, device_id_type=MESH)

    @pl.when(has_left)
    def _():
        pl.semaphore_signal(barrier, inc=1, device_id={"chan": z - 1}, device_id_type=MESH)

    @pl.when(has_right)
    def _():
        pl.semaphore_signal(barrier, inc=1, device_id={"chan": z + 1}, device_id_type=MESH)

    pl.semaphore_wait(barrier, 2 + has_left.astype(jnp.int32) + has_right.astype(jnp.int32))

    def remote(src, dst, send, recv, where):
        return pltpu.make_async_remote_copy(
            src_ref=src, dst_ref=dst, send_sem=send, recv_sem=recv,
            device_id=where, device_id_type=MESH,
        )

    def z_copy(b, right):
        step = 1 if right else -1
        part = slots.at[b, k]
        return remote(part, part, z_send.at[b, int(right)], z_recv.at[b], {"chan": z + step})

    def s_copy(b, seg):
        part = slots.at[b, seg]
        return remote(part, part, s_send.at[b], s_recv.at[b], {"sub": 1 - k})

    def x_copy(b):
        return remote(xsend.at[b], xrecv.at[b], x_send.at[b], x_recv.at[b], {"tm": 1 - x})

    def f_copy(b):
        return remote(fin.at[b], finr.at[b], f_send.at[b], f_recv.at[b], {"sub": 1 - k})

    idx_copy = remote(idx_ref, idx_sib, idx_sems.at[0], idx_sems.at[1], {"sub": 1 - k})
    idx_copy.start()
    idx_copy.wait()

    lane = lax.broadcasted_iota(jnp.int32, (per, resident), 1)
    sel = jnp.zeros((per, resident), jnp.float32)
    for ref in (idx_ref, idx_sib):
        for p in range(2):
            hit = ref[p * per : (p + 1) * per, :] - z * resident == lane
            sel = sel + jnp.where(hit, 1.0, 0.0)
    sel = sel.astype(jnp.bfloat16)
    tile = 1024
    for t in range(0, width, tile):
        slots[z, k, :, t : t + tile] = jnp.dot(
            sel, x_ref[k, :, t : t + tile], preferred_element_type=jnp.float32
        ).astype(jnp.bfloat16)
    slots[z, k, :, width:] = jnp.dot(
        sel, val_ref[k].astype(jnp.float32).astype(jnp.bfloat16), preferred_element_type=jnp.float32
    ).astype(jnp.bfloat16)

    @pl.when(has_left)
    def _():
        z_copy(z, False).start()

    @pl.when(has_right)
    def _():
        z_copy(z, True).start()

    s_copy(z, k).start()

    out_ref[...] = jnp.zeros_like(out_ref)
    wide = lax.broadcasted_iota(jnp.int32, (q, width), 1)
    for seg in range(segs):
        wcols, vcols = [], []
        for half in range(2):
            side = x if half == 0 else 1 - x
            first = pl.multiple_of(side * (2 * q) + k * q, q)
            rec = x_ref[seg, pl.ds(first, q), :].astype(jnp.float32)
            flag = val_ref[seg, pl.ds(first, q), :].astype(jnp.float32)
            mean = jnp.sum(rec * rec, axis=1, keepdims=True) * (1.0 / width)
            w = flag / jnp.sqrt(mean + 1e-05)
            for h in range(REC_SHIFTS):
                by = SRC_SHIFTS * h
                moved = rec
                if by:
                    moved = jnp.where(wide < width - by, pltpu.roll(rec, width - by, 1), 0.0)
                row = (half * REC_SHIFTS + h) * q
                shifted_rec[seg, row : row + q, :] = moved.astype(jnp.bfloat16)
                wcols.append(w)
                vcols.append(flag)
        wrow[seg] = jnp.concatenate(wcols, axis=0).T[:per]
        vrow[seg] = jnp.concatenate(vcols, axis=0).T[:per]

    def compute(b):
        s_copy(b, 1 - k).wait_recv()
        acc = None
        pairs = None
        for seg in range(segs):
            src = slots[b, seg, :, :width].astype(jnp.float32)
            flag = slots[b, seg, :, width:].astype(jnp.float32)
            mean = jnp.sum(src * src, axis=1, keepdims=True) * (1.0 / width)
            a = flag / (math.sqrt(width) * jnp.sqrt(mean + 1e-05))
            a = jnp.concatenate([a, a], axis=1)
            f = jnp.concatenate([flag, flag], axis=1)
            for j in range(SRC_SHIFTS):
                moved = src
                if j:
                    moved = jnp.where(wide[:per] >= j, pltpu.roll(src, j, 1), 0.0)
                shifted_src[seg, j * per : (j + 1) * per, :] = moved.astype(jnp.bfloat16)
            d = lax.dot_general(
                shifted_src[seg], shifted_rec[seg], (((1,), (1,)), ((), ())),
                preferred_element_type=jnp.float32,
            )
            term = d.reshape(SRC_SHIFTS, per, 2 * LANES) * (a * wrow[seg])[None]
            pair = f * vrow[seg]
            acc = term if acc is None else acc + term
            pairs = pair if pairs is None else pairs + pair
        rows = SRC_SHIFTS * per
        own[b, :rows] = acc[:, :, :LANES].reshape(rows, LANES)
        own[b, rows:] = pairs[:, :LANES]
        xsend[b, :rows] = acc[:, :, LANES:].reshape(rows, LANES)
        xsend[b, rows:] = pairs[:, LANES:]
        x_copy(b).start()

    def finish(b):
        x_copy(b).wait_recv()
        rows = SRC_SHIFTS * per
        total = own[b, :rows] + xrecv[b, :rows]
        pairs = own[b, rows:] + xrecv[b, rows:]
        norm = 1.0 / jnp.sqrt(jnp.maximum(pairs, 1.0))
        fin[b] = (total.reshape(SRC_SHIFTS, per, LANES) * norm[None]).reshape(rows, LANES)
        f_copy(b).start()

    def final(b):
        f_copy(b).wait_recv()
        rows = SRC_SHIFTS * per
        mine, other = fin[b], finr[b]
        low = jnp.where(k == 0, mine, other)
        high = jnp.where(k == 0, other, mine)
        at = lax.broadcasted_iota(jnp.int32, (rows, LANES), 1)
        for h in range(REC_SHIFTS):
            lo = pltpu.roll(low, (LANES - h * q) % LANES, 1) if h else low
            hi = pltpu.roll(high, (LANES + q - h * q) % LANES, 1) if h != 1 else high
            both = jnp.where(at < q, lo, hi)[:, : 2 * q]
            both = both.reshape(SRC_SHIFTS, per, 2 * q)
            for p in range(2):
                channel = idx_ref[p * per : (p + 1) * per, : 2 * q]
                held = (channel >= b * resident) & (channel < (b + 1) * resident)
                at_lags = pl.ds(h * SRC_SHIFTS, SRC_SHIFTS)
                at_rows = pl.ds(p * per, per)
                before = out_ref[at_lags, at_rows, :]
                out_ref[at_lags, at_rows, :] = jnp.where(held[None], both, before)

    def item(d, way):
        b = z + d * (2 * way - 1)
        ok = (b >= 0) & (b < n_chan) & (d >= 0) & ((d > 0) | (way == 0))
        return b, ok

    @pl.loop(0, n_chan + 2)
    def _(d):
        from_left, ok_left = item(d, 0)
        from_right, ok_right = item(d, 1)

        @pl.when(ok_left & (d > 0))
        def _():
            z_copy(from_left, True).wait_recv()

            @pl.when(has_right)
            def _():
                z_copy(from_left, True).start()

            s_copy(from_left, k).start()

        @pl.when(ok_right & (d > 0))
        def _():
            z_copy(from_right, False).wait_recv()

            @pl.when(has_left)
            def _():
                z_copy(from_right, False).start()

            s_copy(from_right, k).start()

        @pl.loop(0, 2)
        def _(way):
            b, ok = item(d, way)

            @pl.when(ok)
            def _():
                compute(b)

            b1, ok1 = item(d - 1, way)

            @pl.when(ok1)
            def _():
                finish(b1)

            b2, ok2 = item(d - 2, way)

            @pl.when(ok2)
            def _():
                final(b2)

    @pl.loop(0, n_chan)
    def _(b):
        @pl.when(has_left & (b >= z))
        def _():
            z_copy(b, False).wait_send()

        @pl.when(has_right & (b <= z))
        def _():
            z_copy(b, True).wait_send()

        s_copy(b, k).wait_send()
        x_copy(b).wait_send()
        f_copy(b).wait_send()


def fast_body(n_chan, traces, valid, source_channel_index):
    resident, segs, width = traces.shape
    panels, per = source_channel_index.shape
    x = jnp.transpose(traces, (1, 0, 2))
    idx = jnp.broadcast_to(source_channel_index.reshape(-1)[:, None], (panels * per, LANES))
    val = jnp.broadcast_to(valid.T[:, :, None], (segs, resident, LANES))
    rows = SRC_SHIFTS * per
    vmem = pl.BlockSpec(memory_space=pltpu.VMEM)
    dma = pltpu.SemaphoreType.DMA
    f32, bf16 = jnp.float32, jnp.bfloat16
    return pl.pallas_call(
        functools.partial(kernel, n_chan),
        out_shape=jax.ShapeDtypeStruct((LAGS, panels * per, resident // 2), f32),
        in_specs=[vmem] * 3,
        out_specs=vmem,
        scratch_shapes=[
            pltpu.VMEM((n_chan, segs, per, width + LANES), bf16),
            pltpu.VMEM((panels * per, LANES), jnp.int32),
            pltpu.VMEM((segs, 2 * LANES, width), bf16),
            pltpu.VMEM((segs, rows, width), bf16),
            pltpu.VMEM((segs, per, 2 * LANES), f32),
            pltpu.VMEM((segs, per, 2 * LANES), f32),
            pltpu.VMEM((n_chan, rows + per, LANES), f32),
            pltpu.VMEM((n_chan, rows + per, LANES), f32),
            pltpu.VMEM((n_chan, rows + per, LANES), f32),
            pltpu.VMEM((n_chan, rows, LANES), f32),
            pltpu.VMEM((n_chan, rows, LANES), f32),
            dma((2,)),
            dma((n_chan, 2)),
            dma((n_chan,)),
            dma((n_chan,)),
            dma((n_chan,)),
            dma((n_chan,)),
            dma((n_chan,)),
            dma((n_chan,)),
            dma((n_chan,)),
        ],
        compiler_params=pltpu.CompilerParams(
            collective_id=0, has_side_effects=True, vmem_limit_bytes=48 * 1024 * 1024
        ),
    )(x, idx, val)


def solution(mesh):
    in_specs = (P(("grp", "chan"), "tm", None), P(("grp", "chan"), "tm"), P(("grp", "sub"), None))
    out_specs = P(None, ("grp", "sub"), ("chan", "tm"))
    size = mesh.shape

    def body(traces, valid, source_channel_index):
        panels = source_channel_index.shape[0] * size["sub"]
        fits = (
            (size["tm"], size["sub"], traces.shape[1]) == (2, 2, 2)
            and panels == size["chan"]
            and traces.shape[0] == LANES
            and source_channel_index.shape == (2, LANES // REC_SHIFTS)
        )
        if fits:
            return fast_body(size["chan"], traces, valid, source_channel_index)
        return general_body(traces, valid, source_channel_index)

    return jax.shard_map(body, mesh=mesh, in_specs=in_specs, out_specs=out_specs, check_vma=False)
```

```python
import functools
import math

import jax
import jax.numpy as jnp
from jax import lax
from jax.experimental import pallas as pl
from jax.experimental.pallas import tpu as pltpu
from jax.sharding import PartitionSpec as P

LAGS = 32
SRC_SHIFTS = 8
REC_SHIFTS = LAGS // SRC_SHIFTS
PIECES = 2
LANES = 128
MESH = pl.DeviceIdType.MESH


def from_root(array, axis, root):
    size = lax.axis_size(axis)
    moving = jnp.where(lax.axis_index(axis) == root, array, jnp.zeros_like(array))
    total = moving
    for _ in range(size - 1):
        moving = lax.ppermute(moving, axis, [(i, (i + 1) % size) for i in range(size)])
        total = total + moving
    return total


def sum_to_owners(array, axis, dim):
    size = lax.axis_size(axis)
    part = array.shape[dim] // size
    me = lax.axis_index(axis)

    def piece(owner):
        return lax.dynamic_slice_in_dim(array, owner * part, part, dim)

    total = piece(me)
    for step in range(1, size):
        away = [(i, (i + step) % size) for i in range(size)]
        total = total + lax.ppermute(piece((me + step) % size), axis, away)
    return total


def shifted_block(src, first, count):
    width = src.shape[-1]
    rows = []
    for lag in range(first, first + count):
        rows.append(jnp.pad(src, ((0, 0), (0, 0), (lag, 0)))[:, :, :width])
    return jnp.stack(rows)


def general_body(traces, valid, source_channel_index):
    resident_traces = traces.shape[0]
    seg_here = traces.shape[1]
    width = traces.shape[2]
    panels_here = source_channel_index.shape[0]
    per_panel = source_channel_index.shape[1]
    rms_rec = jnp.sqrt(jnp.mean(jnp.square(traces.astype(jnp.float32)), axis=2) + 1e-05)
    rec_mask = valid.astype(jnp.float32)
    owners = source_channel_index[:, 0] // resident_traces
    local_rows = (source_channel_index - owners[:, None] * resident_traces).reshape(-1)
    chosen = (local_rows[:, None] == jnp.arange(resident_traces)[None, :]).astype(jnp.bfloat16)
    picked = jnp.einsum("nc,ckt->nkt", chosen, traces, preferred_element_type=jnp.float32)
    picked = picked.astype(jnp.bfloat16).reshape(panels_here, per_panel, seg_here, width)
    pick_mask = jnp.dot(chosen, valid.astype(jnp.bfloat16), preferred_element_type=jnp.float32)
    pick_mask = pick_mask.astype(jnp.bfloat16).reshape(panels_here, per_panel, seg_here)

    def fetch(panel):
        return (
            from_root(picked[panel], "chan", owners[panel]),
            from_root(pick_mask[panel], "chan", owners[panel]),
        )

    fetched = [fetch(panel) for panel in range(panels_here)]
    sources = jnp.stack([item[0] for item in fetched])
    src_flags = jnp.stack([item[1] for item in fetched])
    sources = sources.reshape(panels_here * per_panel, seg_here, width)
    src_mask = src_flags.reshape(panels_here * per_panel, seg_here).astype(jnp.float32)
    rms_src = jnp.sqrt(jnp.mean(jnp.square(sources.astype(jnp.float32)), axis=2) + 1e-05)
    scale = (
        src_mask.T[:, :, None]
        * rec_mask.T[:, None, :]
        / (math.sqrt(width) * rms_src.T[:, :, None] * rms_rec.T[:, None, :])
    )
    group = min(8, LAGS)
    blocks = []
    for start in range(0, LAGS, group):
        lag_shifted = shifted_block(sources, start, group)
        lagged_product = jnp.einsum(
            "lsku,rku->klsr", lag_shifted, traces, preferred_element_type=jnp.float32
        )
        blocks.append(jnp.sum(lagged_product * scale[:, None], axis=0))
    partial_stack_value = jnp.concatenate(blocks, axis=0)
    pair_terms = jnp.dot(src_mask, rec_mask.T, preferred_element_type=jnp.float32)
    total = sum_to_owners(partial_stack_value, "tm", 2)
    pairs = sum_to_owners(pair_terms, "tm", 1)
    return total / jnp.sqrt(jnp.maximum(pairs, 1.0))[None]


def kernel(
    n_chan, x_ref, idx_ref, val_ref, out_ref,
    slots, idx_sib, shifted_rec, shifted_src, wrow, vrow, own, xsend, xrecv, fin, finr,
    idx_sems, z_send, z_recv, s_send, s_recv, x_send, x_recv, f_send, f_recv,
):
    segs, resident, width = x_ref.shape
    panel = idx_ref.shape[0] // 2
    per = panel // PIECES
    q = resident // 4
    z = lax.axis_index("chan")
    x = lax.axis_index("tm")
    k = lax.axis_index("sub")
    has_left = z > 0
    has_right = z < n_chan - 1

    barrier = pltpu.get_barrier_semaphore()
    pl.semaphore_signal(barrier, inc=1, device_id={"sub": 1 - k}, device_id_type=MESH)
    pl.semaphore_signal(barrier, inc=1, device_id={"tm": 1 - x}, device_id_type=MESH)

    @pl.when(has_left)
    def _():
        pl.semaphore_signal(barrier, inc=1, device_id={"chan": z - 1}, device_id_type=MESH)

    @pl.when(has_right)
    def _():
        pl.semaphore_signal(barrier, inc=1, device_id={"chan": z + 1}, device_id_type=MESH)

    pl.semaphore_wait(barrier, 2 + has_left.astype(jnp.int32) + has_right.astype(jnp.int32))

    def remote(src, dst, send, recv, where):
        return pltpu.make_async_remote_copy(
            src_ref=src, dst_ref=dst, send_sem=send, recv_sem=recv,
            device_id=where, device_id_type=MESH,
        )

    def z_copy(b, right):
        step = 1 if right else -1
        part = slots.at[b, k]
        return remote(part, part, z_send.at[b, int(right)], z_recv.at[b], {"chan": z + step})

    def s_copy(b, seg):
        part = slots.at[b, seg]
        return remote(part, part, s_send.at[b], s_recv.at[b], {"sub": 1 - k})

    def x_copy(b):
        return remote(xsend.at[b], xrecv.at[b], x_send.at[b], x_recv.at[b], {"tm": 1 - x})

    def f_copy(b):
        return remote(fin.at[b], finr.at[b], f_send.at[b], f_recv.at[b], {"sub": 1 - k})

    idx_copy = remote(idx_ref, idx_sib, idx_sems.at[0], idx_sems.at[1], {"sub": 1 - k})
    idx_copy.start()
    idx_copy.wait()

    lane = lax.broadcasted_iota(jnp.int32, (panel, resident), 1)
    sel = jnp.zeros((panel, resident), jnp.float32)
    for ref in (idx_ref, idx_sib):
        for p in range(2):
            hit = ref[p * panel : (p + 1) * panel, :] - z * resident == lane
            sel = sel + jnp.where(hit, 1.0, 0.0)
    sel = sel.astype(jnp.bfloat16)
    tile = 1024
    def place(rows, at):
        rows = rows.astype(jnp.bfloat16)
        for piece in range(PIECES):
            slots[z * PIECES + piece, k, :, at : at + rows.shape[1]] = rows[piece * per : (piece + 1) * per]

    for t in range(0, width, tile):
        place(jnp.dot(sel, x_ref[k, :, t : t + tile], preferred_element_type=jnp.float32), t)
    place(jnp.dot(sel, val_ref[k].astype(jnp.bfloat16), preferred_element_type=jnp.float32), width)

    for piece in range(PIECES):
        i = z * PIECES + piece

        @pl.when(has_left)
        def _(i=i):
            z_copy(i, False).start()

        @pl.when(has_right)
        def _(i=i):
            z_copy(i, True).start()

        s_copy(i, k).start()

    out_ref[...] = jnp.zeros_like(out_ref)
    wide = lax.broadcasted_iota(jnp.int32, (q, width), 1)
    for seg in range(segs):
        wcols, vcols = [], []
        for half in range(2):
            side = x if half == 0 else 1 - x
            first = pl.multiple_of(side * (2 * q) + k * q, q)
            rec = x_ref[seg, pl.ds(first, q), :].astype(jnp.float32)
            flag = val_ref[seg, pl.ds(first, q), :]
            mean = jnp.sum(rec * rec, axis=1, keepdims=True) * (1.0 / width)
            w = flag / jnp.sqrt(mean + 1e-05)
            for h in range(REC_SHIFTS):
                by = SRC_SHIFTS * h
                moved = rec
                if by:
                    moved = jnp.where(wide < width - by, pltpu.roll(rec, width - by, 1), 0.0)
                row = (half * REC_SHIFTS + h) * q
                shifted_rec[seg, row : row + q, :] = moved.astype(jnp.bfloat16)
                wcols.append(w)
                vcols.append(flag)
        wrow[seg] = jnp.concatenate(wcols, axis=0).T[:per]
        vrow[seg] = jnp.concatenate(vcols, axis=0).T[:per]

    def compute(b):
        s_copy(b, 1 - k).wait_recv()
        acc = None
        pairs = None
        for seg in range(segs):
            src = slots[b, seg, :, :width].astype(jnp.float32)
            flag = slots[b, seg, :, width:].astype(jnp.float32)
            mean = jnp.sum(src * src, axis=1, keepdims=True) * (1.0 / width)
            a = flag / (math.sqrt(width) * jnp.sqrt(mean + 1e-05))
            a = jnp.concatenate([a, a], axis=1)
            f = jnp.concatenate([flag, flag], axis=1)
            for j in range(SRC_SHIFTS):
                moved = src
                if j:
                    moved = jnp.where(wide[:per] >= j, pltpu.roll(src, j, 1), 0.0)
                shifted_src[seg, j * per : (j + 1) * per, :] = moved.astype(jnp.bfloat16)
            d = lax.dot_general(
                shifted_src[seg], shifted_rec[seg], (((1,), (1,)), ((), ())),
                preferred_element_type=jnp.float32,
            )
            term = d.reshape(SRC_SHIFTS, per, 2 * LANES) * (a * wrow[seg])[None]
            pair = f * vrow[seg]
            acc = term if acc is None else acc + term
            pairs = pair if pairs is None else pairs + pair
        rows = SRC_SHIFTS * per
        own[b, :rows] = acc[:, :, :LANES].reshape(rows, LANES)
        own[b, rows:] = pairs[:, :LANES]
        xsend[b, :rows] = acc[:, :, LANES:].reshape(rows, LANES)
        xsend[b, rows:] = pairs[:, LANES:]
        x_copy(b).start()

    def finish(b):
        x_copy(b).wait_recv()
        rows = SRC_SHIFTS * per
        total = own[b, :rows] + xrecv[b, :rows]
        pairs = own[b, rows:] + xrecv[b, rows:]
        norm = 1.0 / jnp.sqrt(jnp.maximum(pairs, 1.0))
        fin[b] = (total.reshape(SRC_SHIFTS, per, LANES) * norm[None]).reshape(rows, LANES)
        f_copy(b).start()

    def final(b):
        f_copy(b).wait_recv()
        block = b // PIECES
        first = pl.multiple_of((b % PIECES) * per, per)
        rows = SRC_SHIFTS * per
        mine, other = fin[b], finr[b]
        low = jnp.where(k == 0, mine, other)
        high = jnp.where(k == 0, other, mine)
        at = lax.broadcasted_iota(jnp.int32, (rows, LANES), 1)
        for h in range(REC_SHIFTS):
            lo = pltpu.roll(low, (LANES - h * q) % LANES, 1) if h else low
            hi = pltpu.roll(high, (LANES + q - h * q) % LANES, 1) if h != 1 else high
            both = jnp.where(at < q, lo, hi)[:, : 2 * q]
            both = both.reshape(SRC_SHIFTS, per, 2 * q)
            for p in range(2):
                channel = idx_ref[pl.ds(p * panel + first, per), :][:, : 2 * q]
                held = (channel >= block * resident) & (channel < (block + 1) * resident)
                at_lags = pl.ds(h * SRC_SHIFTS, SRC_SHIFTS)
                at_rows = pl.ds(p * panel + first, per)
                before = out_ref[at_lags, at_rows, :]
                out_ref[at_lags, at_rows, :] = jnp.where(held[None], both, before)

    def item(e, way):
        d = (e + PIECES) // PIECES - 1
        block = z + d * (2 * way - 1)
        ok = (block >= 0) & (block < n_chan) & (d >= 0) & ((d > 0) | (way == 0))
        return block * PIECES + (e + PIECES) % PIECES, ok

    @pl.loop(0, n_chan * PIECES + 2)
    def _(d):
        from_left, ok_left = item(d, 0)
        from_right, ok_right = item(d, 1)

        @pl.when(ok_left & (d >= PIECES))
        def _():
            z_copy(from_left, True).wait_recv()

            @pl.when(has_right)
            def _():
                z_copy(from_left, True).start()

            s_copy(from_left, k).start()

        @pl.when(ok_right & (d >= PIECES))
        def _():
            z_copy(from_right, False).wait_recv()

            @pl.when(has_left)
            def _():
                z_copy(from_right, False).start()

            s_copy(from_right, k).start()

        @pl.loop(0, 2)
        def _(way):
            b, ok = item(d, way)

            @pl.when(ok)
            def _():
                compute(b)

            b1, ok1 = item(d - 1, way)

            @pl.when(ok1)
            def _():
                finish(b1)

            b2, ok2 = item(d - 2, way)

            @pl.when(ok2)
            def _():
                final(b2)

    @pl.loop(0, n_chan * PIECES)
    def _(b):
        block = b // PIECES

        @pl.when(has_left & (block >= z))
        def _():
            z_copy(b, False).wait_send()

        @pl.when(has_right & (block <= z))
        def _():
            z_copy(b, True).wait_send()

        s_copy(b, k).wait_send()
        x_copy(b).wait_send()
        f_copy(b).wait_send()


def fast_body(n_chan, traces, valid, source_channel_index):
    resident, segs, width = traces.shape
    panels, per = source_channel_index.shape
    part, items = per // PIECES, n_chan * PIECES
    x = jnp.transpose(traces, (1, 0, 2))
    idx = jnp.broadcast_to(source_channel_index.reshape(-1)[:, None], (panels * per, LANES))
    val = jnp.broadcast_to(valid.T.astype(jnp.float32)[:, :, None], (segs, resident, LANES))
    rows = SRC_SHIFTS * part
    vmem = pl.BlockSpec(memory_space=pltpu.VMEM)
    dma = pltpu.SemaphoreType.DMA
    f32, bf16 = jnp.float32, jnp.bfloat16
    return pl.pallas_call(
        functools.partial(kernel, n_chan),
        out_shape=jax.ShapeDtypeStruct((LAGS, panels * per, resident // 2), f32),
        in_specs=[vmem] * 3,
        out_specs=vmem,
        scratch_shapes=[
            pltpu.VMEM((items, segs, part, width + LANES), bf16),
            pltpu.VMEM((panels * per, LANES), jnp.int32),
            pltpu.VMEM((segs, 2 * LANES, width), bf16),
            pltpu.VMEM((segs, rows, width), bf16),
            pltpu.VMEM((segs, part, 2 * LANES), f32),
            pltpu.VMEM((segs, part, 2 * LANES), f32),
            pltpu.VMEM((items, rows + part, LANES), f32),
            pltpu.VMEM((items, rows + part, LANES), f32),
            pltpu.VMEM((items, rows + part, LANES), f32),
            pltpu.VMEM((items, rows, LANES), f32),
            pltpu.VMEM((items, rows, LANES), f32),
            dma((2,)),
            dma((items, 2)),
            dma((items,)),
            dma((items,)),
            dma((items,)),
            dma((items,)),
            dma((items,)),
            dma((items,)),
            dma((items,)),
        ],
        compiler_params=pltpu.CompilerParams(
            collective_id=0, has_side_effects=True, vmem_limit_bytes=48 * 1024 * 1024
        ),
    )(x, idx, val)


def solution(mesh):
    in_specs = (P(("grp", "chan"), "tm", None), P(("grp", "chan"), "tm"), P(("grp", "sub"), None))
    out_specs = P(None, ("grp", "sub"), ("chan", "tm"))
    size = mesh.shape

    def body(traces, valid, source_channel_index):
        panels = source_channel_index.shape[0] * size["sub"]
        fits = (
            (size["tm"], size["sub"], traces.shape[1]) == (2, 2, 2)
            and panels == size["chan"]
            and traces.shape[0] == LANES
            and source_channel_index.shape == (2, LANES // REC_SHIFTS)
        )
        if fits:
            return fast_body(size["chan"], traces, valid, source_channel_index)
        return general_body(traces, valid, source_channel_index)

    return jax.shard_map(body, mesh=mesh, in_specs=in_specs, out_specs=out_specs, check_vma=False)
```

```python
import functools
import math

import jax
import jax.numpy as jnp
from jax import lax
from jax.experimental import pallas as pl
from jax.experimental.pallas import tpu as pltpu
from jax.sharding import PartitionSpec as P

LAGS = 32
SRC_SHIFTS = 8
REC_SHIFTS = LAGS // SRC_SHIFTS
PIECES = 2
LANES = 128
MESH = pl.DeviceIdType.MESH


def from_root(array, axis, root):
    size = lax.axis_size(axis)
    moving = jnp.where(lax.axis_index(axis) == root, array, jnp.zeros_like(array))
    total = moving
    for _ in range(size - 1):
        moving = lax.ppermute(moving, axis, [(i, (i + 1) % size) for i in range(size)])
        total = total + moving
    return total


def sum_to_owners(array, axis, dim):
    size = lax.axis_size(axis)
    part = array.shape[dim] // size
    me = lax.axis_index(axis)

    def piece(owner):
        return lax.dynamic_slice_in_dim(array, owner * part, part, dim)

    total = piece(me)
    for step in range(1, size):
        away = [(i, (i + step) % size) for i in range(size)]
        total = total + lax.ppermute(piece((me + step) % size), axis, away)
    return total


def shifted_block(src, first, count):
    width = src.shape[-1]
    rows = []
    for lag in range(first, first + count):
        rows.append(jnp.pad(src, ((0, 0), (0, 0), (lag, 0)))[:, :, :width])
    return jnp.stack(rows)


def general_body(traces, valid, source_channel_index):
    resident_traces = traces.shape[0]
    seg_here = traces.shape[1]
    width = traces.shape[2]
    panels_here = source_channel_index.shape[0]
    per_panel = source_channel_index.shape[1]
    rms_rec = jnp.sqrt(jnp.mean(jnp.square(traces.astype(jnp.float32)), axis=2) + 1e-05)
    rec_mask = valid.astype(jnp.float32)
    owners = source_channel_index[:, 0] // resident_traces
    local_rows = (source_channel_index - owners[:, None] * resident_traces).reshape(-1)
    chosen = (local_rows[:, None] == jnp.arange(resident_traces)[None, :]).astype(jnp.bfloat16)
    picked = jnp.einsum("nc,ckt->nkt", chosen, traces, preferred_element_type=jnp.float32)
    picked = picked.astype(jnp.bfloat16).reshape(panels_here, per_panel, seg_here, width)
    pick_mask = jnp.dot(chosen, valid.astype(jnp.bfloat16), preferred_element_type=jnp.float32)
    pick_mask = pick_mask.astype(jnp.bfloat16).reshape(panels_here, per_panel, seg_here)

    def fetch(panel):
        return (
            from_root(picked[panel], "chan", owners[panel]),
            from_root(pick_mask[panel], "chan", owners[panel]),
        )

    fetched = [fetch(panel) for panel in range(panels_here)]
    sources = jnp.stack([item[0] for item in fetched])
    src_flags = jnp.stack([item[1] for item in fetched])
    sources = sources.reshape(panels_here * per_panel, seg_here, width)
    src_mask = src_flags.reshape(panels_here * per_panel, seg_here).astype(jnp.float32)
    rms_src = jnp.sqrt(jnp.mean(jnp.square(sources.astype(jnp.float32)), axis=2) + 1e-05)
    scale = (
        src_mask.T[:, :, None]
        * rec_mask.T[:, None, :]
        / (math.sqrt(width) * rms_src.T[:, :, None] * rms_rec.T[:, None, :])
    )
    group = min(8, LAGS)
    blocks = []
    for start in range(0, LAGS, group):
        lag_shifted = shifted_block(sources, start, group)
        lagged_product = jnp.einsum(
            "lsku,rku->klsr", lag_shifted, traces, preferred_element_type=jnp.float32
        )
        blocks.append(jnp.sum(lagged_product * scale[:, None], axis=0))
    partial_stack_value = jnp.concatenate(blocks, axis=0)
    pair_terms = jnp.dot(src_mask, rec_mask.T, preferred_element_type=jnp.float32)
    total = sum_to_owners(partial_stack_value, "tm", 2)
    pairs = sum_to_owners(pair_terms, "tm", 1)
    return total / jnp.sqrt(jnp.maximum(pairs, 1.0))[None]


def kernel(
    n_chan, x_ref, idx_ref, val_ref, out_ref,
    slots, idx_sib, shifted_rec, shifted_src, wrow, vrow, own, xsend, xrecv, fin, finr,
    idx_sems, z_send, z_recv, s_send, s_recv, x_send, x_recv, f_send, f_recv,
):
    segs, resident, width = x_ref.shape
    panel = idx_ref.shape[0] // 2
    per = panel // PIECES
    q = resident // 4
    z = lax.axis_index("chan")
    x = lax.axis_index("tm")
    k = lax.axis_index("sub")
    has_left = z > 0
    has_right = z < n_chan - 1

    barrier = pltpu.get_barrier_semaphore()
    pl.semaphore_signal(barrier, inc=1, device_id={"sub": 1 - k}, device_id_type=MESH)
    pl.semaphore_signal(barrier, inc=1, device_id={"tm": 1 - x}, device_id_type=MESH)

    @pl.when(has_left)
    def _():
        pl.semaphore_signal(barrier, inc=1, device_id={"chan": z - 1}, device_id_type=MESH)

    @pl.when(has_right)
    def _():
        pl.semaphore_signal(barrier, inc=1, device_id={"chan": z + 1}, device_id_type=MESH)

    pl.semaphore_wait(barrier, 2 + has_left.astype(jnp.int32) + has_right.astype(jnp.int32))

    def remote(src, dst, send, recv, where):
        return pltpu.make_async_remote_copy(
            src_ref=src, dst_ref=dst, send_sem=send, recv_sem=recv,
            device_id=where, device_id_type=MESH,
        )

    def z_copy(b, right):
        step = 1 if right else -1
        part = slots.at[b, k]
        return remote(part, part, z_send.at[b, int(right)], z_recv.at[b], {"chan": z + step})

    def s_copy(b, seg):
        part = slots.at[b, seg]
        return remote(part, part, s_send.at[b], s_recv.at[b], {"sub": 1 - k})

    def x_copy(b):
        return remote(xsend.at[b], xrecv.at[b], x_send.at[b], x_recv.at[b], {"tm": 1 - x})

    def f_copy(b):
        return remote(fin.at[b], finr.at[b], f_send.at[b], f_recv.at[b], {"sub": 1 - k})

    idx_copy = remote(idx_ref, idx_sib, idx_sems.at[0], idx_sems.at[1], {"sub": 1 - k})
    idx_copy.start()
    idx_copy.wait()

    lane = lax.broadcasted_iota(jnp.int32, (panel, resident), 1)
    sel = jnp.zeros((panel, resident), jnp.float32)
    for ref in (idx_ref, idx_sib):
        for p in range(2):
            hit = ref[p * panel : (p + 1) * panel, :] - z * resident == lane
            sel = sel + jnp.where(hit, 1.0, 0.0)
    sel = sel.astype(jnp.bfloat16)
    tile = 1024
    def place(rows, at):
        rows = rows.astype(jnp.bfloat16)
        for piece in range(PIECES):
            slots[z * PIECES + piece, k, :, at : at + rows.shape[1]] = rows[piece * per : (piece + 1) * per]

    for t in range(0, width, tile):
        place(jnp.dot(sel, x_ref[k, :, t : t + tile], preferred_element_type=jnp.float32), t)
    place(jnp.dot(sel, val_ref[k].astype(jnp.bfloat16), preferred_element_type=jnp.float32), width)

    for piece in range(PIECES):
        i = z * PIECES + piece

        @pl.when(has_left)
        def _(i=i):
            z_copy(i, False).start()

        @pl.when(has_right)
        def _(i=i):
            z_copy(i, True).start()

        s_copy(i, k).start()

    out_ref[...] = jnp.zeros_like(out_ref)
    wide = lax.broadcasted_iota(jnp.int32, (q, width), 1)
    for seg in range(segs):
        wcols, vcols = [], []
        for half in range(2):
            side = x if half == 0 else 1 - x
            first = pl.multiple_of(side * (2 * q) + k * q, q)
            rec = x_ref[seg, pl.ds(first, q), :].astype(jnp.float32)
            flag = val_ref[seg, pl.ds(first, q), :]
            mean = jnp.sum(rec * rec, axis=1, keepdims=True) * (1.0 / width)
            w = flag / jnp.sqrt(mean + 1e-05)
            turned = []
            for h in range(REC_SHIFTS):
                by = SRC_SHIFTS * h
                moved = rec
                if by:
                    moved = jnp.where(wide < width - by, pltpu.roll(rec, width - by, 1), 0.0)
                turned.append(moved.astype(jnp.bfloat16))
                wcols.append(w)
                vcols.append(flag)
            shifted_rec[seg, :, half * LANES : (half + 1) * LANES] = jnp.concatenate(turned, axis=0).T
        wrow[seg] = jnp.concatenate(wcols, axis=0).T[:per]
        vrow[seg] = jnp.concatenate(vcols, axis=0).T[:per]

    def compute(b):
        s_copy(b, 1 - k).wait_recv()
        acc = None
        pairs = None
        for seg in range(segs):
            src = slots[b, seg, :, :width].astype(jnp.float32)
            flag = slots[b, seg, :, width:].astype(jnp.float32)
            mean = jnp.sum(src * src, axis=1, keepdims=True) * (1.0 / width)
            a = flag / (math.sqrt(width) * jnp.sqrt(mean + 1e-05))
            a = jnp.concatenate([a, a], axis=1)
            f = jnp.concatenate([flag, flag], axis=1)
            for j in range(SRC_SHIFTS):
                moved = src
                if j:
                    moved = jnp.where(wide[:per] >= j, pltpu.roll(src, j, 1), 0.0)
                shifted_src[seg, j * per : (j + 1) * per, :] = moved.astype(jnp.bfloat16)
            d = lax.dot_general(
                shifted_src[seg], shifted_rec[seg], (((1,), (0,)), ((), ())),
                preferred_element_type=jnp.float32,
            )
            term = d.reshape(SRC_SHIFTS, per, 2 * LANES) * (a * wrow[seg])[None]
            pair = f * vrow[seg]
            acc = term if acc is None else acc + term
            pairs = pair if pairs is None else pairs + pair
        rows = SRC_SHIFTS * per
        own[b, :rows] = acc[:, :, :LANES].reshape(rows, LANES)
        own[b, rows:] = pairs[:, :LANES]
        xsend[b, :rows] = acc[:, :, LANES:].reshape(rows, LANES)
        xsend[b, rows:] = pairs[:, LANES:]
        x_copy(b).start()

    def finish(b):
        x_copy(b).wait_recv()
        rows = SRC_SHIFTS * per
        total = own[b, :rows] + xrecv[b, :rows]
        pairs = own[b, rows:] + xrecv[b, rows:]
        norm = 1.0 / jnp.sqrt(jnp.maximum(pairs, 1.0))
        fin[b] = (total.reshape(SRC_SHIFTS, per, LANES) * norm[None]).reshape(rows, LANES)
        f_copy(b).start()

    def final(b):
        f_copy(b).wait_recv()
        block = b // PIECES
        first = pl.multiple_of((b % PIECES) * per, per)
        rows = SRC_SHIFTS * per
        mine, other = fin[b], finr[b]
        low = jnp.where(k == 0, mine, other)
        high = jnp.where(k == 0, other, mine)
        at = lax.broadcasted_iota(jnp.int32, (rows, LANES), 1)
        for h in range(REC_SHIFTS):
            lo = pltpu.roll(low, (LANES - h * q) % LANES, 1) if h else low
            hi = pltpu.roll(high, (LANES + q - h * q) % LANES, 1) if h != 1 else high
            both = jnp.where(at < q, lo, hi)[:, : 2 * q]
            both = both.reshape(SRC_SHIFTS, per, 2 * q)
            for p in range(2):
                channel = idx_ref[pl.ds(p * panel + first, per), :][:, : 2 * q]
                held = (channel >= block * resident) & (channel < (block + 1) * resident)
                at_lags = pl.ds(h * SRC_SHIFTS, SRC_SHIFTS)
                at_rows = pl.ds(p * panel + first, per)
                before = out_ref[at_lags, at_rows, :]
                out_ref[at_lags, at_rows, :] = jnp.where(held[None], both, before)

    def item(e, way):
        d = (e + PIECES) // PIECES - 1
        block = z + d * (2 * way - 1)
        ok = (block >= 0) & (block < n_chan) & (d >= 0) & ((d > 0) | (way == 0))
        return block * PIECES + (e + PIECES) % PIECES, ok

    @pl.loop(0, n_chan * PIECES + 2)
    def _(d):
        from_left, ok_left = item(d, 0)
        from_right, ok_right = item(d, 1)

        @pl.when(ok_left & (d >= PIECES))
        def _():
            z_copy(from_left, True).wait_recv()

            @pl.when(has_right)
            def _():
                z_copy(from_left, True).start()

            s_copy(from_left, k).start()

        @pl.when(ok_right & (d >= PIECES))
        def _():
            z_copy(from_right, False).wait_recv()

            @pl.when(has_left)
            def _():
                z_copy(from_right, False).start()

            s_copy(from_right, k).start()

        @pl.loop(0, 2)
        def _(way):
            b, ok = item(d, way)

            @pl.when(ok)
            def _():
                compute(b)

            b1, ok1 = item(d - 1, way)

            @pl.when(ok1)
            def _():
                finish(b1)

            b2, ok2 = item(d - 2, way)

            @pl.when(ok2)
            def _():
                final(b2)

    @pl.loop(0, n_chan * PIECES)
    def _(b):
        block = b // PIECES

        @pl.when(has_left & (block >= z))
        def _():
            z_copy(b, False).wait_send()

        @pl.when(has_right & (block <= z))
        def _():
            z_copy(b, True).wait_send()

        s_copy(b, k).wait_send()
        x_copy(b).wait_send()
        f_copy(b).wait_send()


def fast_body(n_chan, traces, valid, source_channel_index):
    resident, segs, width = traces.shape
    panels, per = source_channel_index.shape
    part, items = per // PIECES, n_chan * PIECES
    x = jnp.transpose(traces, (1, 0, 2))
    idx = jnp.broadcast_to(source_channel_index.reshape(-1)[:, None], (panels * per, LANES))
    val = jnp.broadcast_to(valid.T.astype(jnp.float32)[:, :, None], (segs, resident, LANES))
    rows = SRC_SHIFTS * part
    vmem = pl.BlockSpec(memory_space=pltpu.VMEM)
    dma = pltpu.SemaphoreType.DMA
    f32, bf16 = jnp.float32, jnp.bfloat16
    return pl.pallas_call(
        functools.partial(kernel, n_chan),
        out_shape=jax.ShapeDtypeStruct((LAGS, panels * per, resident // 2), f32),
        in_specs=[vmem] * 3,
        out_specs=vmem,
        scratch_shapes=[
            pltpu.VMEM((items, segs, part, width + LANES), bf16),
            pltpu.VMEM((panels * per, LANES), jnp.int32),
            pltpu.VMEM((segs, width, 2 * LANES), bf16),
            pltpu.VMEM((segs, rows, width), bf16),
            pltpu.VMEM((segs, part, 2 * LANES), f32),
            pltpu.VMEM((segs, part, 2 * LANES), f32),
            pltpu.VMEM((items, rows + part, LANES), f32),
            pltpu.VMEM((items, rows + part, LANES), f32),
            pltpu.VMEM((items, rows + part, LANES), f32),
            pltpu.VMEM((items, rows, LANES), f32),
            pltpu.VMEM((items, rows, LANES), f32),
            dma((2,)),
            dma((items, 2)),
            dma((items,)),
            dma((items,)),
            dma((items,)),
            dma((items,)),
            dma((items,)),
            dma((items,)),
            dma((items,)),
        ],
        compiler_params=pltpu.CompilerParams(
            collective_id=0, has_side_effects=True, vmem_limit_bytes=48 * 1024 * 1024
        ),
    )(x, idx, val)


def solution(mesh):
    in_specs = (P(("grp", "chan"), "tm", None), P(("grp", "chan"), "tm"), P(("grp", "sub"), None))
    out_specs = P(None, ("grp", "sub"), ("chan", "tm"))
    size = mesh.shape

    def body(traces, valid, source_channel_index):
        panels = source_channel_index.shape[0] * size["sub"]
        fits = (
            (size["tm"], size["sub"], traces.shape[1]) == (2, 2, 2)
            and panels == size["chan"]
            and traces.shape[0] == LANES
            and source_channel_index.shape == (2, LANES // REC_SHIFTS)
        )
        if fits:
            return fast_body(size["chan"], traces, valid, source_channel_index)
        return general_body(traces, valid, source_channel_index)

    return jax.shard_map(body, mesh=mesh, in_specs=in_specs, out_specs=out_specs, check_vma=False)
```
